32 devices in a mesh: elec: 8 (over z, y), space: 4 (over x, core).
Axes of the slice: x: 2, y: 2, z: 4, core: 2. Of those that a mesh axis runs over, the one named last changes fastest.
Arguments:
- sigma_real: float32 [8, 64, 128], P('space'), may hold values from 0.3 to 3
- sigma_imag: float32 [8, 64, 128], P('space'), may hold values from -0.5 to 0.5
- warm_fields: float32 [32, 2, 8, 64, 128], P('elec', None, 'space'), may hold values from -6 to 6
- locations: int32 [32], P('elec'), may hold values from 0 to 65535
- counts: int32 [8], P('elec'), may hold values from 1 to 48, 128 in all
- quads: int32 [8, 48, 4], P('elec'), may hold values from 0 to 31
Outputs:
- jacobian: bfloat16 [128, 2, 8, 64, 128], P('elec', None, 'space')
The draws below stay inside these ranges and needn't reach their ends.
Inputs may be any that keep to these rules, and one draw needn't show every extreme that they name: The counts sum to 128; group h's measurements are its first counts[h] slots. `quads`: slots past a group's count are unused.
All inputs are finite; a program needn't handle non-finite values.
Results may differ from the reference program's by a relative error of at most 0.0072.
Values may be sent and summed in bfloat16 or wider, within the bound.
A program may use at most 128 MiB of HBM per device.

```python
import math
import jax
import jax.numpy as jnp
import numpy as np
from jax import lax

NY = 64
NZ = 128
MEASURE_ROWS_MEAN = 16
ITERS = 2
MEASURE_SLOTS = 48
ELECTRODE_TOTAL = 32
MEASURE_ROWS = 128
NX = 8
N_ELEC = 8


def set_ends(entries, rng, low, high):
    spot = [jax.random.randint(jax.random.fold_in(rng, axis), (), 0, length) for axis, length in enumerate(entries.shape)]
    main_axis = entries.shape.index(max(entries.shape))
    neighbour = spot[:main_axis] + [(spot[main_axis] + 1) % entries.shape[main_axis]] + spot[main_axis + 1:]
    return entries.at[tuple(spot)].set(low).at[tuple(neighbour)].set(high)


def levels(stream_key, extent, pieces, low, top_value):
    def one(position, blocks):
        steps = jax.random.uniform(jax.random.fold_in(jax.random.fold_in(stream_key, 6), position), (blocks,), jnp.float32, low / len(pieces), top_value / len(pieces))
        return jnp.repeat(jnp.exp(steps), extent[position] // blocks).reshape((-1,) + (1,) * (len(extent) - position - 1))

    loudness = one(*pieces[0])
    for cut in pieces[1:]:
        loudness = loudness * one(*cut)
    return loudness


def profile(count, total, bound, skew):
    portions = [(1 << 20) // math.isqrt(rank ** skew) + 1 for rank in range(2, count + 1)]
    spare, given = total - bound - (count - 1), [1] * (count - 1)
    while spare > 0:
        candidates = [i for i in range(count - 1) if given[i] < bound]
        mass, left = sum([portions[i] for i in candidates]), spare
        for i in candidates:
            more = min(bound - given[i], max(1, left * portions[i] // mass), spare)
            given[i] = given[i] + more
            spare = spare - more
    return np.array([bound] + given)


def uneven_parts(own_key, amount, total, bound, lean):
    if amount == 2:
        one = jax.random.randint(own_key, (), max(1, total - bound), min(bound, total - 1) + 1)
        return jnp.stack([one, total - one])
    tallies = jnp.asarray(profile(amount, total, bound, lean), jnp.int32)
    pairs = (amount - 1) // 2
    source_of, taker = tallies[1:1 + 2 * pairs:2], tallies[2:2 + 2 * pairs:2]
    room = jnp.minimum(source_of - 1, bound - taker)
    shifted = jax.random.randint(jax.random.fold_in(own_key, 1), (pairs,), 0, 1 << 20) % (room + 1)
    tallies = tallies.at[1:1 + 2 * pairs:2].set(source_of - shifted).at[2:2 + 2 * pairs:2].set(taker + shifted)
    return tallies[jax.random.permutation(jax.random.fold_in(own_key, 2), amount)]


def gaussian(key, shape, scale, limit, pieces=(), held_as=jnp.bfloat16):
    entries = scale * jax.random.normal(key, shape, jnp.float32)
    if pieces:
        entries = entries * levels(key, shape, pieces, -0.22, 0.18)
    return jnp.clip(entries, -limit, limit).astype(held_as)


def setup_inputs(seed: int = 0) -> dict:
    splits = jax.random.split(jax.random.key(seed), 7)
    sigma_real = jnp.clip(jnp.exp(math.log(3.0) - 2.3025851 * jax.random.uniform(splits[0], (NX, NY, NZ), jnp.float32) ** levels(splits[0], (NX, NY, NZ), ((0, 4),), -0.2, 0.2)), 0.3, 3.0)
    sigma_imag = jnp.clip(jax.random.uniform(splits[1], (NX, NY, NZ), jnp.float32, -0.5, 0.5) * levels(splits[1], (NX, NY, NZ), ((0, 4),), -0.4, 0.0), -0.5, 0.5)
    warm_fields = gaussian(splits[2], (ELECTRODE_TOTAL, 2, NX, NY, NZ), 1.0, 6.0, ((0, 8), (2, 4)), jnp.float32)
    locations = set_ends(jax.random.randint(splits[3], (ELECTRODE_TOTAL,), 0, NX * NY * NZ), jax.random.fold_in(splits[3], 1), 0, (NX * NY * NZ) - 1).astype(jnp.int32)
    counts = uneven_parts(splits[4], N_ELEC, MEASURE_ROWS, MEASURE_SLOTS, 2).astype(jnp.int32)
    quads = set_ends(jax.random.randint(splits[5], (N_ELEC, MEASURE_SLOTS, 4), 0, ELECTRODE_TOTAL), jax.random.fold_in(splits[5], 1), 0, ELECTRODE_TOTAL - 1).astype(jnp.int32)
    return {"sigma_real": sigma_real, "sigma_imag": sigma_imag, "warm_fields": warm_fields, "locations": locations, "counts": counts, "quads": quads}


screen = 0.3
current = 4.0


def relax_weights():
    spread_half = 6.0 / (6.0 + screen)
    return [1.0 / (1.0 + spread_half * math.cos(math.pi * (2 * k + 1) / (2 * ITERS))) for k in range(ITERS)]


def neighbour_total(field):
    padded = jnp.pad(field, ((0, 0), (1, 1), (1, 1), (1, 1)))
    total = padded[:, 2:, 1:-1, 1:-1] + padded[:, :-2, 1:-1, 1:-1]
    total = total + padded[:, 1:-1, 2:, 1:-1] + padded[:, 1:-1, :-2, 1:-1]
    total = total + padded[:, 1:-1, 1:-1, 2:] + padded[:, 1:-1, 1:-1, :-2]
    return total


def gradients_of(potential):
    values = lax.optimization_barrier(potential).astype(jnp.float32)
    padded = jnp.pad(values, ((0, 0), (1, 1), (1, 1), (1, 1)))
    grad_x = (padded[:, 2:, 1:-1, 1:-1] - padded[:, :-2, 1:-1, 1:-1]) * 0.5
    grad_y = (padded[:, 1:-1, 2:, 1:-1] - padded[:, 1:-1, :-2, 1:-1]) * 0.5
    grad_z = (padded[:, 1:-1, 1:-1, 2:] - padded[:, 1:-1, 1:-1, :-2]) * 0.5
    return jnp.stack([grad_x, grad_y, grad_z], axis=1).astype(jnp.bfloat16)


def reference(sigma_real, sigma_imag, warm_fields, locations, counts, quads):
    nx, ny, nz = sigma_real.shape
    x_index = lax.broadcasted_iota(jnp.int32, (nx, ny, nz), 0)
    y_index = lax.broadcasted_iota(jnp.int32, (nx, ny, nz), 1)
    z_index = lax.broadcasted_iota(jnp.int32, (nx, ny, nz), 2)
    flat_index = (x_index * ny + y_index) * nz + z_index
    inverse = 1.0 / ((6.0 + screen) * (sigma_real * sigma_real + sigma_imag * sigma_imag))
    weights = relax_weights()

    def solve_one(pair):
        warm, place = pair
        strength = jnp.where(flat_index == place, jnp.float32(current), jnp.float32(0.0))
        source = jnp.stack([strength * sigma_real * inverse, -(strength * sigma_imag * inverse)], axis=0)
        field = warm
        for iteration in range(ITERS):
            field = field + weights[iteration] * (source - field + neighbour_total(field) / (6.0 + screen))
        return gradients_of(field.astype(jnp.bfloat16))

    gradient_table = lax.map(solve_one, (warm_fields, locations))
    ends = jnp.cumsum(counts).astype(jnp.int32)
    starts = (ends - counts).astype(jnp.int32)
    row_total = MEASURE_ROWS_MEAN * N_ELEC
    row_indices = jnp.arange(row_total, dtype=jnp.int32)
    owners = jnp.sum((ends[None, :] <= row_indices[:, None]).astype(jnp.int32), axis=1).astype(jnp.int32)
    slot_ids = (row_indices - starts[owners]).astype(jnp.int32)
    chosen = quads[owners, slot_ids]

    def one_row(quad):
        pair_source = gradient_table[quad[0]].astype(jnp.float32) - gradient_table[quad[1]].astype(jnp.float32)
        pair_probe = gradient_table[quad[2]].astype(jnp.float32) - gradient_table[quad[3]].astype(jnp.float32)
        dot_real = jnp.sum(pair_source[0] * pair_probe[0] - pair_source[1] * pair_probe[1], axis=0)
        dot_imag = jnp.sum(pair_source[0] * pair_probe[1] + pair_source[1] * pair_probe[0], axis=0)
        part_real = -(sigma_real * dot_real - sigma_imag * dot_imag)
        part_imag = -(sigma_real * dot_imag + sigma_imag * dot_real)
        return jnp.stack([part_real, part_imag], axis=0).astype(jnp.bfloat16)

    return lax.map(one_row, chosen)
```

```python
import functools
import math

import jax
import jax.numpy as jnp
from jax import lax
from jax.experimental import pallas as pl
from jax.experimental.pallas import tpu as pltpu
from jax.sharding import PartitionSpec as P

MEASURE_ROWS_MEAN = 16
ITERS = 2

screen = 0.3
current = 4.0

MESH = pl.DeviceIdType.MESH
F32 = jnp.float32
BF16 = jnp.bfloat16


def relax_weights(count):
    spread_half = 6.0 / (6.0 + screen)
    return [
        1.0 / (1.0 + spread_half * math.cos(math.pi * (2 * k + 1) / (2 * count)))
        for k in range(count)
    ]


def shifted(v, dim, step):
    size = v.shape[dim]
    index = lax.broadcasted_iota(jnp.int32, v.shape, dim)
    if step > 0:
        return jnp.where(index == 0, 0.0, pltpu.roll(v, 1, dim))
    return jnp.where(index == size - 1, 0.0, pltpu.roll(v, size - 1, dim))


def in_plane(v):
    return (
        shifted(v, 0, 1) + shifted(v, 0, -1) + shifted(v, 1, 1) + shifted(v, 1, -1)
    )


def kernel(
    n,
    spaces,
    slots,
    sig_r,
    sig_i,
    warm,
    loc,
    ints,
    out,
    pot,
    q,
    partial,
    halo_out,
    halo_in,
    gathered_ints,
    ints_smem,
    halo_send,
    halo_recv,
    ring_send,
    ring_recv,
    side_send,
    side_recv,
    int_send,
    int_recv,
    local_sem,
):
    half = n // 2
    w0, w1 = relax_weights(ITERS)
    elec = lax.axis_index("elec")
    space = lax.axis_index("space")
    even = lax.rem(elec, 2) == 0
    place = jnp.where(even, elec // 2, n - 1 - elec // 2)

    def elec_at(p):
        p = lax.rem(p + 2 * n, n)
        return jnp.where(p < half, 2 * p, 2 * (n - 1 - p) + 1)

    ahead, behind = elec_at(place + 1), elec_at(place - 1)
    has_left, has_right = space > 0, space < spaces - 1
    per = warm.shape[0]
    ny, nz = warm.shape[3], warm.shape[4]

    barrier = pltpu.get_barrier_semaphore()
    for o in range(1, n):
        pl.semaphore_signal(
            barrier, inc=1, device_id=(lax.rem(elec + o, n), space), device_id_type=MESH
        )

    @pl.when(has_left)
    def _():
        pl.semaphore_signal(barrier, inc=1, device_id=(elec, space - 1), device_id_type=MESH)

    @pl.when(has_right)
    def _():
        pl.semaphore_signal(barrier, inc=1, device_id=(elec, space + 1), device_id_type=MESH)

    for x in range(2):
        sr, si = sig_r[x], sig_i[x]
        inverse = current / ((6.0 + screen) * (sr * sr + si * si))
        q[0, x] = sr * inverse
        q[1, x] = -(si * inverse)

    y_index = lax.broadcasted_iota(jnp.int32, (ny, nz), 0)
    z_index = lax.broadcasted_iota(jnp.int32, (ny, nz), 1)
    cell = y_index * nz + z_index

    def source(e, part, x):
        flat = cell + (space * 2 + x) * (ny * nz)
        return jnp.where(flat == loc[e], q[part, x], 0.0)

    def first(i, carry):
        e = i // 2
        part = i - 2 * e
        for x in range(2):
            f = warm[e, part, x]
            other = warm[e, part, 1 - x]
            value = (
                (1.0 - w0) * f
                + w0 * source(e, part, x)
                + (w0 / (6.0 + screen)) * (in_plane(f) + other)
            )
            partial[i, x] = value
            halo_out[x, 0, i] = f.astype(BF16)
            halo_out[x, 1, i] = value.astype(BF16)
        return carry

    lax.fori_loop(0, 2 * per, first, 0)

    @pl.when(jnp.logical_not(has_left))
    def _():
        halo_in[0] = jnp.zeros(halo_in.shape[1:], BF16)
        for o in range(n):
            pot[o, 0] = jnp.zeros(pot.shape[2:], BF16)

    @pl.when(jnp.logical_not(has_right))
    def _():
        halo_in[1] = jnp.zeros(halo_in.shape[1:], BF16)
        for o in range(n):
            pot[o, 3] = jnp.zeros(pot.shape[2:], BF16)

    neighbours = jnp.where(has_left, 1, 0) + jnp.where(has_right, 1, 0)
    pl.semaphore_wait(barrier, n - 1 + neighbours)

    def warm_copy(side):
        return pltpu.make_async_remote_copy(
            src_ref=halo_out.at[side],
            dst_ref=halo_in.at[1 - side],
            send_sem=halo_send.at[side],
            recv_sem=halo_recv.at[1 - side],
            device_id=(elec, space - 1 if side == 0 else space + 1),
            device_id_type=MESH,
        )

    def warm_arrival(side):
        return pltpu.make_async_remote_copy(
            src_ref=halo_out.at[side],
            dst_ref=halo_in.at[side],
            send_sem=halo_send.at[side],
            recv_sem=halo_recv.at[side],
            device_id=(elec, space),
            device_id_type=MESH,
        )

    present = (has_left, has_right)
    for side in range(2):

        @pl.when(present[side])
        def _():
            warm_copy(side).start()

    def int_copy(o):
        return pltpu.make_async_remote_copy(
            src_ref=ints,
            dst_ref=gathered_ints.at[n - o],
            send_sem=int_send.at[o],
            recv_sem=int_recv.at[n - o],
            device_id=(lax.rem(elec + o, n), space),
            device_id_type=MESH,
        )

    for o in range(1, n):
        int_copy(o).start()

    for side in range(2):

        @pl.when(present[side])
        def _():
            warm_arrival(side).wait_recv()

    left_on = jnp.where(has_left, 1.0, 0.0).astype(F32)
    right_on = jnp.where(has_right, 1.0, 0.0).astype(F32)

    def second(i, carry):
        e = i // 2
        part = i - 2 * e
        c0 = w0 / (6.0 + screen)
        c1 = w1 / (6.0 + screen)
        warm_left = halo_in[0, 0, i].astype(F32)
        warm_right = halo_in[1, 0, i].astype(F32)
        low = partial[i, 0] + c0 * warm_left
        high = partial[i, 1] + c0 * warm_right
        left = halo_in[0, 1, i].astype(F32) + (c0 * left_on) * warm[e, part, 0]
        right = halo_in[1, 1, i].astype(F32) + (c0 * right_on) * warm[e, part, 1]
        pot[0, 1, i] = (
            (1.0 - w1) * low + w1 * source(e, part, 0) + c1 * (in_plane(low) + high + left)
        ).astype(BF16)
        pot[0, 2, i] = (
            (1.0 - w1) * high + w1 * source(e, part, 1) + c1 * (in_plane(high) + low + right)
        ).astype(BF16)
        return carry

    lax.fori_loop(0, 2 * per, second, 0)

    def ring_copy(way, o, x):
        src = o if way == 0 else (n - o) % n
        dst = o + 1 if way == 0 else n - o - 1
        return pltpu.make_async_remote_copy(
            src_ref=pot.at[src, 1 + x],
            dst_ref=pot.at[dst, 1 + x],
            send_sem=ring_send.at[way, o, x],
            recv_sem=ring_recv.at[way, o, x],
            device_id=(ahead if way == 0 else behind, space),
            device_id_type=MESH,
        )

    def side_copy(o, x):
        return pltpu.make_async_remote_copy(
            src_ref=pot.at[o, 1 + x],
            dst_ref=pot.at[o, 3 if x == 0 else 0],
            send_sem=side_send.at[o, x],
            recv_sem=side_recv.at[o, x],
            device_id=(elec, space - 1 if x == 0 else space + 1),
            device_id_type=MESH,
        )

    def send_side(o, x):
        @pl.when(present[x])
        def _():
            side_copy(o, x).start()

    def travels(way, o, x):
        return o < half - 1 or (o == half - 1 and x == way)

    for x in range(2):
        for way in range(2):
            if travels(way, 0, x):
                ring_copy(way, 0, x).start()
        send_side(0, x)
    for o in range(1, half + 1):
        for x in range(2):
            for way in range(2):
                if travels(way, o - 1, x):
                    ring_copy(way, o - 1, x).wait_recv()
                    if travels(way, o, x):
                        ring_copy(way, o, x).start()
                    send_side(o if way == 0 else n - o, x)

    for o in range(1, n):
        int_copy(n - o).wait_recv()
    gathered_ints[0] = ints[...]
    local = pltpu.make_async_copy(gathered_ints, ints_smem, local_sem)
    local.start()
    local.wait()

    for o in range(n):
        for x in range(2):

            @pl.when(present[1 - x])
            def _():
                side_copy(o, x).wait_recv()

    lanes = ints.shape[1]

    def row(r, carry):
        number = elec * MEASURE_ROWS_MEAN + r
        end = jnp.int32(0)
        start = jnp.int32(0)
        owner = jnp.int32(0)
        for g in range(n):
            where = lax.rem(g - elec + n, n)
            end = end + ints_smem[where, slots * 4 // lanes, slots * 4 % lanes]
            passed = end <= number
            owner = owner + jnp.where(passed, 1, 0)
            start = jnp.where(passed, end, start)
        slot = number - start
        where = lax.rem(owner - elec + n, n)

        def chosen(j):
            at = slot * 4 + j
            e = ints_smem[where, at // lanes, lax.rem(at, lanes)]
            h = e // per
            p = jnp.where(lax.rem(h, 2) == 0, h // 2, n - 1 - h // 2)
            return lax.rem(place - p + n, n), 2 * (e - h * per)

        picks = [chosen(j) for j in range(4)]

        def pair(k, part, x):
            (oa, ea), (ob, eb) = picks[2 * k], picks[2 * k + 1]
            return pot[oa, x, ea + part].astype(F32) - pot[ob, x, eb + part].astype(F32)

        for x in range(2):
            grads = []
            for k in range(2):
                parts = []
                for part in range(2):
                    v = pair(k, part, 1 + x)
                    parts.append(
                        (
                            pair(k, part, 2 + x) - pair(k, part, x),
                            shifted(v, 0, -1) - shifted(v, 0, 1),
                            shifted(v, 1, -1) - shifted(v, 1, 1),
                        )
                    )
                grads.append(parts)
            (s_re, s_im), (p_re, p_im) = grads
            dot_re = sum(s_re[c] * p_re[c] - s_im[c] * p_im[c] for c in range(3))
            dot_im = sum(s_re[c] * p_im[c] + s_im[c] * p_re[c] for c in range(3))
            sr, si = -0.25 * sig_r[x], -0.25 * sig_i[x]
            out[r, 0, x] = (sr * dot_re - si * dot_im).astype(BF16)
            out[r, 1, x] = (sr * dot_im + si * dot_re).astype(BF16)
        return carry

    lax.fori_loop(0, MEASURE_ROWS_MEAN, row, 0)

    for side in range(2):

        @pl.when(present[side])
        def _():
            warm_copy(side).wait_send()
            for o in range(n):
                side_copy(o, side).wait_send()

    for o in range(1, n):
        int_copy(o).wait_send()
    for o in range(half):
        for x in range(2):
            for way in range(2):
                if travels(way, o, x):
                    ring_copy(way, o, x).wait_send()


def per_device(n, spaces, sigma_real, sigma_imag, warm_fields, locations, counts, quads):
    per, parts, width, ny, nz = warm_fields.shape
    slots = quads.shape[1]
    fields = per * parts
    flat = jnp.concatenate([quads.reshape(-1), counts])
    flat = jnp.pad(flat, (0, 1024 - flat.shape[0])).reshape(8, 128)
    vmem = pl.BlockSpec(memory_space=pltpu.VMEM)
    smem = pl.BlockSpec(memory_space=pltpu.SMEM)
    half = n // 2
    dma = pltpu.SemaphoreType.DMA
    return pl.pallas_call(
        functools.partial(kernel, n, spaces, slots),
        out_shape=jax.ShapeDtypeStruct((MEASURE_ROWS_MEAN, 2, width, ny, nz), BF16),
        in_specs=[vmem, vmem, vmem, smem, vmem],
        out_specs=vmem,
        scratch_shapes=[
            pltpu.VMEM((n, width + 2, fields, ny, nz), BF16),
            pltpu.VMEM((2, width, ny, nz), F32),
            pltpu.VMEM((fields, width, ny, nz), F32),
            pltpu.VMEM((2, 2, fields, ny, nz), BF16),
            pltpu.VMEM((2, 2, fields, ny, nz), BF16),
            pltpu.VMEM((n, 8, 128), jnp.int32),
            pltpu.SMEM((n, 8, 128), jnp.int32),
            dma((2,)),
            dma((2,)),
            dma((2, half, 2)),
            dma((2, half, 2)),
            dma((n, 2)),
            dma((n, 2)),
            dma((n,)),
            dma((n,)),
            dma,
        ],
        compiler_params=pltpu.CompilerParams(
            collective_id=0, has_side_effects=True, vmem_limit_bytes=40 * 1024 * 1024
        ),
    )(sigma_real, sigma_imag, warm_fields, locations, flat)


def solution(mesh):
    in_specs = (
        P("space", None, None),
        P("space", None, None),
        P("elec", None, "space", None, None),
        P("elec"),
        P("elec"),
        P("elec", None, None),
    )
    out_specs = P("elec", None, "space", None, None)
    return jax.shard_map(
        functools.partial(per_device, mesh.shape["elec"], mesh.shape["space"]),
        mesh=mesh,
        in_specs=in_specs,
        out_specs=out_specs,
        check_vma=False,
    )
```

```python
import functools
import math

import jax
import jax.numpy as jnp
from jax import lax
from jax.experimental import pallas as pl
from jax.experimental.pallas import tpu as pltpu
from jax.sharding import PartitionSpec as P

MEASURE_ROWS_MEAN = 16
ITERS = 2

screen = 0.3
current = 4.0

MESH = pl.DeviceIdType.MESH
F32 = jnp.float32
BF16 = jnp.bfloat16


def relax_weights(count):
    spread_half = 6.0 / (6.0 + screen)
    return [
        1.0 / (1.0 + spread_half * math.cos(math.pi * (2 * k + 1) / (2 * count)))
        for k in range(count)
    ]


def shifted(v, dim, step):
    size = v.shape[dim]
    index = lax.broadcasted_iota(jnp.int32, v.shape, dim)
    if step > 0:
        return jnp.where(index == 0, 0.0, pltpu.roll(v, 1, dim))
    return jnp.where(index == size - 1, 0.0, pltpu.roll(v, size - 1, dim))


def in_plane(v):
    return (
        shifted(v, 0, 1) + shifted(v, 0, -1) + shifted(v, 1, 1) + shifted(v, 1, -1)
    )


def kernel(
    n,
    spaces,
    slots,
    sig_r_hbm,
    sig_i_hbm,
    warm_hbm,
    quads_hbm,
    loc,
    count,
    out,
    sig_r,
    sig_i,
    warm,
    quads,
    ints,
    pot,
    q,
    partial,
    halo_out,
    halo_in,
    gathered_ints,
    ints_smem,
    picks,
    table,
    rows_out,
    halo_send,
    halo_recv,
    ring_send,
    ring_recv,
    side_send,
    side_recv,
    int_send,
    int_recv,
    load_sem,
    local_sem,
    out_sem,
):
    half = n // 2
    w0, w1 = relax_weights(ITERS)
    elec = lax.axis_index("elec")
    space = lax.axis_index("space")
    even = lax.rem(elec, 2) == 0
    place = jnp.where(even, elec // 2, n - 1 - elec // 2)

    def elec_at(p):
        p = lax.rem(p + 2 * n, n)
        return jnp.where(p < half, 2 * p, 2 * (n - 1 - p) + 1)

    ahead, behind = elec_at(place + 1), elec_at(place - 1)
    has_left, has_right = space > 0, space < spaces - 1
    per = warm.shape[0]
    ny, nz = warm.shape[3], warm.shape[4]

    loads = [
        pltpu.make_async_copy(a, b, load_sem.at[k])
        for k, (a, b) in enumerate(
            [(warm_hbm, warm), (sig_r_hbm, sig_r), (sig_i_hbm, sig_i), (quads_hbm, quads)]
        )
    ]
    for load in loads:
        load.start()

    barrier = pltpu.get_barrier_semaphore()
    for o in range(1, n):
        pl.semaphore_signal(
            barrier, inc=1, device_id=(lax.rem(elec + o, n), space), device_id_type=MESH
        )

    @pl.when(has_left)
    def _():
        pl.semaphore_signal(barrier, inc=1, device_id=(elec, space - 1), device_id_type=MESH)

    @pl.when(has_right)
    def _():
        pl.semaphore_signal(barrier, inc=1, device_id=(elec, space + 1), device_id_type=MESH)

    @pl.when(jnp.logical_not(has_left))
    def _():
        halo_in[0] = jnp.zeros(halo_in.shape[1:], BF16)
        for o in range(n):
            pot[o, 0] = jnp.zeros(pot.shape[2:], BF16)

    @pl.when(jnp.logical_not(has_right))
    def _():
        halo_in[1] = jnp.zeros(halo_in.shape[1:], BF16)
        for o in range(n):
            pot[o, 3] = jnp.zeros(pot.shape[2:], BF16)

    for load in loads:
        load.wait()
    ints[...] = jnp.zeros(ints.shape, jnp.int32)
    ints[0:4, 0:slots] = quads[0]
    ints[4:5, :] = jnp.full((1, ints.shape[1]), count[0], jnp.int32)

    for x in range(2):
        sr, si = sig_r[x], sig_i[x]
        inverse = current / ((6.0 + screen) * (sr * sr + si * si))
        q[0, x] = sr * inverse
        q[1, x] = -(si * inverse)

    y_index = lax.broadcasted_iota(jnp.int32, (ny, nz), 0)
    z_index = lax.broadcasted_iota(jnp.int32, (ny, nz), 1)
    cell = y_index * nz + z_index

    def source(e, part, x):
        flat = cell + (space * 2 + x) * (ny * nz)
        return jnp.where(flat == loc[e], q[part, x], 0.0)

    def first(i, carry):
        e = i // 2
        part = i - 2 * e
        for x in range(2):
            f = warm[e, part, x]
            other = warm[e, part, 1 - x]
            value = (
                (1.0 - w0) * f
                + w0 * source(e, part, x)
                + (w0 / (6.0 + screen)) * (in_plane(f) + other)
            )
            partial[i, x] = value
            halo_out[x, 0, i] = f.astype(BF16)
            halo_out[x, 1, i] = value.astype(BF16)
        return carry

    lax.fori_loop(0, 2 * per, first, 0)

    neighbours = jnp.where(has_left, 1, 0) + jnp.where(has_right, 1, 0)
    pl.semaphore_wait(barrier, n - 1 + neighbours)

    def warm_copy(side):
        return pltpu.make_async_remote_copy(
            src_ref=halo_out.at[side],
            dst_ref=halo_in.at[1 - side],
            send_sem=halo_send.at[side],
            recv_sem=halo_recv.at[1 - side],
            device_id=(elec, space - 1 if side == 0 else space + 1),
            device_id_type=MESH,
        )

    def warm_arrival(side):
        return pltpu.make_async_remote_copy(
            src_ref=halo_out.at[side],
            dst_ref=halo_in.at[side],
            send_sem=halo_send.at[side],
            recv_sem=halo_recv.at[side],
            device_id=(elec, space),
            device_id_type=MESH,
        )

    present = (has_left, has_right)
    for side in range(2):

        @pl.when(present[side])
        def _():
            warm_copy(side).start()

    def int_copy(o):
        return pltpu.make_async_remote_copy(
            src_ref=ints,
            dst_ref=gathered_ints.at[n - o],
            send_sem=int_send.at[o],
            recv_sem=int_recv.at[n - o],
            device_id=(lax.rem(elec + o, n), space),
            device_id_type=MESH,
        )

    for o in range(1, n):
        int_copy(o).start()

    for side in range(2):

        @pl.when(present[side])
        def _():
            warm_arrival(side).wait_recv()

    left_on = jnp.where(has_left, 1.0, 0.0).astype(F32)
    right_on = jnp.where(has_right, 1.0, 0.0).astype(F32)

    def second(i, carry):
        e = i // 2
        part = i - 2 * e
        c0 = w0 / (6.0 + screen)
        c1 = w1 / (6.0 + screen)
        warm_left = halo_in[0, 0, i].astype(F32)
        warm_right = halo_in[1, 0, i].astype(F32)
        low = partial[i, 0] + c0 * warm_left
        high = partial[i, 1] + c0 * warm_right
        left = halo_in[0, 1, i].astype(F32) + (c0 * left_on) * warm[e, part, 0]
        right = halo_in[1, 1, i].astype(F32) + (c0 * right_on) * warm[e, part, 1]
        pot[0, 1, i] = (
            (1.0 - w1) * low + w1 * source(e, part, 0) + c1 * (in_plane(low) + high + left)
        ).astype(BF16)
        pot[0, 2, i] = (
            (1.0 - w1) * high + w1 * source(e, part, 1) + c1 * (in_plane(high) + low + right)
        ).astype(BF16)
        return carry

    lax.fori_loop(0, 2 * per, second, 0)

    def ring_copy(way, o, x):
        src = o if way == 0 else (n - o) % n
        dst = o + 1 if way == 0 else n - o - 1
        return pltpu.make_async_remote_copy(
            src_ref=pot.at[src, 1 + x],
            dst_ref=pot.at[dst, 1 + x],
            send_sem=ring_send.at[way, o, x],
            recv_sem=ring_recv.at[way, o, x],
            device_id=(ahead if way == 0 else behind, space),
            device_id_type=MESH,
        )

    def side_copy(o, x):
        return pltpu.make_async_remote_copy(
            src_ref=pot.at[o, 1 + x],
            dst_ref=pot.at[o, 3 if x == 0 else 0],
            send_sem=side_send.at[o, x],
            recv_sem=side_recv.at[o, x],
            device_id=(elec, space - 1 if x == 0 else space + 1),
            device_id_type=MESH,
        )

    def send_side(o, x):
        @pl.when(present[x])
        def _():
            side_copy(o, x).start()

    def travels(way, o, x):
        return o < half - 1 or (o == half - 1 and x == way)

    def wait_sides(o):
        for x in range(2):

            @pl.when(present[1 - x])
            def _():
                side_copy(o, x).wait_recv()

    def gradients(o):
        def one(i, carry):
            planes = [pot[o, k, i].astype(F32) for k in range(4)]
            for x in range(2):
                v = planes[1 + x]
                table[o, i, x, 0] = ((planes[2 + x] - planes[x]) * 0.5).astype(BF16)
                table[o, i, x, 1] = ((shifted(v, 0, -1) - shifted(v, 0, 1)) * 0.5).astype(BF16)
                table[o, i, x, 2] = ((shifted(v, 1, -1) - shifted(v, 1, 1)) * 0.5).astype(BF16)
            return carry

        lax.fori_loop(0, 2 * per, one, 0)

    def choose(r, carry):
        number = elec * MEASURE_ROWS_MEAN + r
        end = jnp.int32(0)
        start = jnp.int32(0)
        owner = jnp.int32(0)
        for g in range(n):
            where = lax.rem(g - elec + n, n)
            end = end + ints_smem[where, 4, 0]
            passed = end <= number
            owner = owner + jnp.where(passed, 1, 0)
            start = jnp.where(passed, end, start)
        slot = number - start
        where = lax.rem(owner - elec + n, n)
        for j in range(4):
            e = ints_smem[where, j, slot]
            h = e // per
            p = jnp.where(lax.rem(h, 2) == 0, h // 2, n - 1 - h // 2)
            picks[r, 2 * j] = lax.rem(place - p + n, n)
            picks[r, 2 * j + 1] = 2 * (e - h * per)
        return carry

    def row_copy(r):
        return pltpu.make_async_copy(rows_out.at[r], out.at[r], out_sem.at[r])

    for x in range(2):
        for way in range(2):
            if travels(way, 0, x):
                ring_copy(way, 0, x).start()
        send_side(0, x)

    for o in range(1, n):
        int_copy(n - o).wait_recv()
    gathered_ints[0] = ints[...]
    local = pltpu.make_async_copy(gathered_ints, ints_smem, local_sem)
    local.start()
    local.wait()
    lax.fori_loop(0, MEASURE_ROWS_MEAN, choose, 0)

    for o in range(1, half + 1):
        for x in range(2):
            for way in range(2):
                if travels(way, o - 1, x):
                    ring_copy(way, o - 1, x).wait_recv()
                    if travels(way, o, x):
                        ring_copy(way, o, x).start()
                    send_side(o if way == 0 else n - o, x)
        for done in sorted({o - 1, (n - o + 1) % n}):
            wait_sides(done)
            gradients(done)

    wait_sides(half)
    gradients(half)

    def row(r, carry):
        at = [(picks[r, 2 * j], picks[r, 2 * j + 1]) for j in range(4)]

        def pair(k, part, x, c):
            (oa, ea), (ob, eb) = at[2 * k], at[2 * k + 1]
            return table[oa, ea + part, x, c].astype(F32) - table[ob, eb + part, x, c].astype(F32)

        for x in range(2):
            dot_re = dot_im = 0.0
            for c in range(3):
                s_re, s_im = pair(0, 0, x, c), pair(0, 1, x, c)
                p_re, p_im = pair(1, 0, x, c), pair(1, 1, x, c)
                dot_re = dot_re + (s_re * p_re - s_im * p_im)
                dot_im = dot_im + (s_re * p_im + s_im * p_re)
            sr, si = sig_r[x], sig_i[x]
            rows_out[r, 0, x] = (si * dot_im - sr * dot_re).astype(BF16)
            rows_out[r, 1, x] = (-(sr * dot_im + si * dot_re)).astype(BF16)
        row_copy(r).start()
        return carry

    lax.fori_loop(0, MEASURE_ROWS_MEAN, row, 0)

    for side in range(2):

        @pl.when(present[side])
        def _():
            warm_copy(side).wait_send()
            for o in range(n):
                side_copy(o, side).wait_send()

    for o in range(1, n):
        int_copy(o).wait_send()
    for o in range(half):
        for x in range(2):
            for way in range(2):
                if travels(way, o, x):
                    ring_copy(way, o, x).wait_send()

    def finish(r, carry):
        row_copy(r).wait()
        return carry

    lax.fori_loop(0, MEASURE_ROWS_MEAN, finish, 0)


def per_device(n, spaces, sigma_real, sigma_imag, warm_fields, locations, counts, quads):
    per, parts, width, ny, nz = warm_fields.shape
    slots = quads.shape[1]
    fields = per * parts
    hbm = pl.BlockSpec(memory_space=pltpu.HBM)
    smem = pl.BlockSpec(memory_space=pltpu.SMEM)
    half = n // 2
    dma = pltpu.SemaphoreType.DMA
    return pl.pallas_call(
        functools.partial(kernel, n, spaces, slots),
        out_shape=jax.ShapeDtypeStruct((MEASURE_ROWS_MEAN, 2, width, ny, nz), BF16),
        in_specs=[hbm, hbm, hbm, hbm, smem, smem],
        out_specs=hbm,
        scratch_shapes=[
            pltpu.VMEM((width, ny, nz), F32),
            pltpu.VMEM((width, ny, nz), F32),
            pltpu.VMEM(warm_fields.shape, F32),
            pltpu.VMEM((1, 4, slots), jnp.int32),
            pltpu.VMEM((8, 128), jnp.int32),
            pltpu.VMEM((n, width + 2, fields, ny, nz), BF16),
            pltpu.VMEM((2, width, ny, nz), F32),
            pltpu.VMEM((fields, width, ny, nz), F32),
            pltpu.VMEM((2, 2, fields, ny, nz), BF16),
            pltpu.VMEM((2, 2, fields, ny, nz), BF16),
            pltpu.VMEM((n, 8, 128), jnp.int32),
            pltpu.SMEM((n, 8, 128), jnp.int32),
            pltpu.SMEM((MEASURE_ROWS_MEAN, 8), jnp.int32),
            pltpu.VMEM((n, fields, width, 3, ny, nz), BF16),
            pltpu.VMEM((MEASURE_ROWS_MEAN, 2, width, ny, nz), BF16),
            dma((2,)),
            dma((2,)),
            dma((2, half, 2)),
            dma((2, half, 2)),
            dma((n, 2)),
            dma((n, 2)),
            dma((n,)),
            dma((n,)),
            dma((4,)),
            dma,
            dma((MEASURE_ROWS_MEAN,)),
        ],
        compiler_params=pltpu.CompilerParams(
            collective_id=0, has_side_effects=True, vmem_limit_bytes=60 * 1024 * 1024
        ),
    )(sigma_real, sigma_imag, warm_fields, quads.transpose(0, 2, 1), locations, counts)


def solution(mesh):
    in_specs = (
        P("space", None, None),
        P("space", None, None),
        P("elec", None, "space", None, None),
        P("elec"),
        P("elec"),
        P("elec", None, None),
    )
    out_specs = P("elec", None, "space", None, None)
    return jax.shard_map(
        functools.partial(per_device, mesh.shape["elec"], mesh.shape["space"]),
        mesh=mesh,
        in_specs=in_specs,
        out_specs=out_specs,
        check_vma=False,
    )
```

```python
import functools
import math

import jax
import jax.numpy as jnp
from jax import lax
from jax.experimental import pallas as pl
from jax.experimental.pallas import tpu as pltpu
from jax.sharding import PartitionSpec as P

MEASURE_ROWS_MEAN = 16
ITERS = 2

screen = 0.3
current = 4.0

MESH = pl.DeviceIdType.MESH
F32 = jnp.float32
BF16 = jnp.bfloat16


def relax_weights(count):
    spread_half = 6.0 / (6.0 + screen)
    return [
        1.0 / (1.0 + spread_half * math.cos(math.pi * (2 * k + 1) / (2 * count)))
        for k in range(count)
    ]


def shifted(v, dim, step):
    size = v.shape[dim]
    index = lax.broadcasted_iota(jnp.int32, v.shape, dim)
    if step > 0:
        return jnp.where(index == 0, 0.0, pltpu.roll(v, 1, dim))
    return jnp.where(index == size - 1, 0.0, pltpu.roll(v, size - 1, dim))


def in_plane(v):
    return (
        shifted(v, 0, 1) + shifted(v, 0, -1) + shifted(v, 1, 1) + shifted(v, 1, -1)
    )


def kernel(
    n,
    spaces,
    slots,
    sig_r_hbm,
    sig_i_hbm,
    warm_hbm,
    quads_hbm,
    loc,
    count,
    out,
    sig_r,
    sig_i,
    warm,
    quads,
    ints,
    pot,
    q,
    partial,
    halo_out,
    halo_in,
    gathered_ints,
    ints_smem,
    picks,
    table,
    halo_send,
    halo_recv,
    ring_send,
    ring_recv,
    side_send,
    side_recv,
    int_send,
    int_recv,
    load_sem,
    local_sem,
):
    half = n // 2
    w0, w1 = relax_weights(ITERS)
    elec = lax.axis_index("elec")
    space = lax.axis_index("space")
    even = lax.rem(elec, 2) == 0
    place = jnp.where(even, elec // 2, n - 1 - elec // 2)

    def elec_at(p):
        p = lax.rem(p + 2 * n, n)
        return jnp.where(p < half, 2 * p, 2 * (n - 1 - p) + 1)

    ahead, behind = elec_at(place + 1), elec_at(place - 1)
    has_left, has_right = space > 0, space < spaces - 1
    per = warm.shape[0]
    ny, nz = warm.shape[3], warm.shape[4]

    loads = [
        pltpu.make_async_copy(a, b, load_sem.at[k])
        for k, (a, b) in enumerate(
            [(warm_hbm, warm), (sig_r_hbm, sig_r), (sig_i_hbm, sig_i), (quads_hbm, quads)]
        )
    ]
    for load in loads:
        load.start()

    barrier = pltpu.get_barrier_semaphore()
    for o in range(1, n):
        pl.semaphore_signal(
            barrier, inc=1, device_id=(lax.rem(elec + o, n), space), device_id_type=MESH
        )

    @pl.when(has_left)
    def _():
        pl.semaphore_signal(barrier, inc=1, device_id=(elec, space - 1), device_id_type=MESH)

    @pl.when(has_right)
    def _():
        pl.semaphore_signal(barrier, inc=1, device_id=(elec, space + 1), device_id_type=MESH)

    @pl.when(jnp.logical_not(has_left))
    def _():
        halo_in[0] = jnp.zeros(halo_in.shape[1:], BF16)
        for o in range(n):
            pot[o, 0] = jnp.zeros(pot.shape[2:], BF16)

    @pl.when(jnp.logical_not(has_right))
    def _():
        halo_in[1] = jnp.zeros(halo_in.shape[1:], BF16)
        for o in range(n):
            pot[o, 3] = jnp.zeros(pot.shape[2:], BF16)

    for load in loads:
        load.wait()
    ints[...] = jnp.zeros(ints.shape, jnp.int32)
    ints[0:4, 0:slots] = quads[0]
    ints[4:5, :] = jnp.full((1, ints.shape[1]), count[0], jnp.int32)

    for x in range(2):
        sr, si = sig_r[x], sig_i[x]
        inverse = current / ((6.0 + screen) * (sr * sr + si * si))
        q[0, x] = sr * inverse
        q[1, x] = -(si * inverse)

    y_index = lax.broadcasted_iota(jnp.int32, (ny, nz), 0)
    z_index = lax.broadcasted_iota(jnp.int32, (ny, nz), 1)
    cell = y_index * nz + z_index

    def source(e, part, x):
        flat = cell + (space * 2 + x) * (ny * nz)
        return jnp.where(flat == loc[e], q[part, x], 0.0)

    def first(i, carry):
        e = i // 2
        part = i - 2 * e
        for x in range(2):
            f = warm[e, part, x]
            other = warm[e, part, 1 - x]
            value = (
                (1.0 - w0) * f
                + w0 * source(e, part, x)
                + (w0 / (6.0 + screen)) * (in_plane(f) + other)
            )
            partial[i, x] = value
            halo_out[x, 0, i] = f.astype(BF16)
            halo_out[x, 1, i] = value.astype(BF16)
        return carry

    lax.fori_loop(0, 2 * per, first, 0)

    neighbours = jnp.where(has_left, 1, 0) + jnp.where(has_right, 1, 0)
    pl.semaphore_wait(barrier, n - 1 + neighbours)

    def warm_copy(side):
        return pltpu.make_async_remote_copy(
            src_ref=halo_out.at[side],
            dst_ref=halo_in.at[1 - side],
            send_sem=halo_send.at[side],
            recv_sem=halo_recv.at[1 - side],
            device_id=(elec, space - 1 if side == 0 else space + 1),
            device_id_type=MESH,
        )

    def warm_arrival(side):
        return pltpu.make_async_remote_copy(
            src_ref=halo_out.at[side],
            dst_ref=halo_in.at[side],
            send_sem=halo_send.at[side],
            recv_sem=halo_recv.at[side],
            device_id=(elec, space),
            device_id_type=MESH,
        )

    present = (has_left, has_right)
    for side in range(2):

        @pl.when(present[side])
        def _():
            warm_copy(side).start()

    def int_copy(o):
        return pltpu.make_async_remote_copy(
            src_ref=ints,
            dst_ref=gathered_ints.at[n - o],
            send_sem=int_send.at[o],
            recv_sem=int_recv.at[n - o],
            device_id=(lax.rem(elec + o, n), space),
            device_id_type=MESH,
        )

    for o in range(1, n):
        int_copy(o).start()

    for side in range(2):

        @pl.when(present[side])
        def _():
            warm_arrival(side).wait_recv()

    left_on = jnp.where(has_left, 1.0, 0.0).astype(F32)
    right_on = jnp.where(has_right, 1.0, 0.0).astype(F32)

    def second(i, carry):
        e = i // 2
        part = i - 2 * e
        c0 = w0 / (6.0 + screen)
        c1 = w1 / (6.0 + screen)
        warm_left = halo_in[0, 0, i].astype(F32)
        warm_right = halo_in[1, 0, i].astype(F32)
        low = partial[i, 0] + c0 * warm_left
        high = partial[i, 1] + c0 * warm_right
        left = halo_in[0, 1, i].astype(F32) + (c0 * left_on) * warm[e, part, 0]
        right = halo_in[1, 1, i].astype(F32) + (c0 * right_on) * warm[e, part, 1]
        pot[0, 1, i] = (
            (1.0 - w1) * low + w1 * source(e, part, 0) + c1 * (in_plane(low) + high + left)
        ).astype(BF16)
        pot[0, 2, i] = (
            (1.0 - w1) * high + w1 * source(e, part, 1) + c1 * (in_plane(high) + low + right)
        ).astype(BF16)
        return carry

    lax.fori_loop(0, 2 * per, second, 0)

    def ring_copy(way, o, x):
        src = o if way == 0 else (n - o) % n
        dst = o + 1 if way == 0 else n - o - 1
        return pltpu.make_async_remote_copy(
            src_ref=pot.at[src, 1 + x],
            dst_ref=pot.at[dst, 1 + x],
            send_sem=ring_send.at[way, o, x],
            recv_sem=ring_recv.at[way, o, x],
            device_id=(ahead if way == 0 else behind, space),
            device_id_type=MESH,
        )

    def side_copy(o, x):
        return pltpu.make_async_remote_copy(
            src_ref=pot.at[o, 1 + x],
            dst_ref=pot.at[o, 3 if x == 0 else 0],
            send_sem=side_send.at[o, x],
            recv_sem=side_recv.at[o, x],
            device_id=(elec, space - 1 if x == 0 else space + 1),
            device_id_type=MESH,
        )

    def send_side(o, x):
        @pl.when(present[x])
        def _():
            side_copy(o, x).start()

    def travels(way, o, x):
        return o < half - 1 or (o == half - 1 and x == way)

    def wait_sides(o):
        for x in range(2):

            @pl.when(present[1 - x])
            def _():
                side_copy(o, x).wait_recv()

    def gradients(o):
        def one(i, carry):
            planes = [pot[o, k, i].astype(F32) for k in range(4)]
            for x in range(2):
                v = planes[1 + x]
                table[o, i, x, 0] = ((planes[2 + x] - planes[x]) * 0.5).astype(BF16)
                table[o, i, x, 1] = ((shifted(v, 0, -1) - shifted(v, 0, 1)) * 0.5).astype(BF16)
                table[o, i, x, 2] = ((shifted(v, 1, -1) - shifted(v, 1, 1)) * 0.5).astype(BF16)
            return carry

        lax.fori_loop(0, 2 * per, one, 0)

    def choose(r, carry):
        number = elec * MEASURE_ROWS_MEAN + r
        end = jnp.int32(0)
        start = jnp.int32(0)
        owner = jnp.int32(0)
        for g in range(n):
            where = lax.rem(g - elec + n, n)
            end = end + ints_smem[where, 4, 0]
            passed = end <= number
            owner = owner + jnp.where(passed, 1, 0)
            start = jnp.where(passed, end, start)
        slot = number - start
        where = lax.rem(owner - elec + n, n)
        for j in range(4):
            e = ints_smem[where, j, slot]
            h = e // per
            p = jnp.where(lax.rem(h, 2) == 0, h // 2, n - 1 - h // 2)
            picks[r, 2 * j] = lax.rem(place - p + n, n)
            picks[r, 2 * j + 1] = 2 * (e - h * per)
        return carry

    for x in range(2):
        for way in range(2):
            if travels(way, 0, x):
                ring_copy(way, 0, x).start()
        send_side(0, x)

    for o in range(1, n):
        int_copy(n - o).wait_recv()
    gathered_ints[0] = ints[...]
    local = pltpu.make_async_copy(gathered_ints, ints_smem, local_sem)
    local.start()
    local.wait()
    lax.fori_loop(0, MEASURE_ROWS_MEAN, choose, 0)

    for o in range(1, half + 1):
        for x in range(2):
            for way in range(2):
                if travels(way, o - 1, x):
                    ring_copy(way, o - 1, x).wait_recv()
                    if travels(way, o, x):
                        ring_copy(way, o, x).start()
                    send_side(o if way == 0 else n - o, x)
        for done in sorted({o - 1, (n - o + 1) % n}):
            wait_sides(done)
            gradients(done)

    wait_sides(half)
    gradients(half)

    def row(r, carry):
        at = [(picks[r, 2 * j], picks[r, 2 * j + 1]) for j in range(4)]

        def pair(k, part, x, c):
            (oa, ea), (ob, eb) = at[2 * k], at[2 * k + 1]
            return table[oa, ea + part, x, c].astype(F32) - table[ob, eb + part, x, c].astype(F32)

        for x in range(2):
            dot_re = dot_im = 0.0
            for c in range(3):
                s_re, s_im = pair(0, 0, x, c), pair(0, 1, x, c)
                p_re, p_im = pair(1, 0, x, c), pair(1, 1, x, c)
                dot_re = dot_re + (s_re * p_re - s_im * p_im)
                dot_im = dot_im + (s_re * p_im + s_im * p_re)
            sr, si = sig_r[x], sig_i[x]
            out[r, 0, x] = (si * dot_im - sr * dot_re).astype(BF16)
            out[r, 1, x] = (-(sr * dot_im + si * dot_re)).astype(BF16)
        return carry

    lax.fori_loop(0, MEASURE_ROWS_MEAN, row, 0)

    for side in range(2):

        @pl.when(present[side])
        def _():
            warm_copy(side).wait_send()
            for o in range(n):
                side_copy(o, side).wait_send()

    for o in range(1, n):
        int_copy(o).wait_send()
    for o in range(half):
        for x in range(2):
            for way in range(2):
                if travels(way, o, x):
                    ring_copy(way, o, x).wait_send()


def per_device(n, spaces, sigma_real, sigma_imag, warm_fields, locations, counts, quads):
    per, parts, width, ny, nz = warm_fields.shape
    slots = quads.shape[1]
    fields = per * parts
    hbm = pl.BlockSpec(memory_space=pltpu.HBM)
    smem = pl.BlockSpec(memory_space=pltpu.SMEM)
    half = n // 2
    dma = pltpu.SemaphoreType.DMA
    return pl.pallas_call(
        functools.partial(kernel, n, spaces, slots),
        out_shape=pltpu.VMEM((MEASURE_ROWS_MEAN, 2, width, ny, nz), BF16),
        in_specs=[hbm, hbm, hbm, hbm, smem, smem],
        out_specs=pl.BlockSpec(memory_space=pltpu.VMEM),
        scratch_shapes=[
            pltpu.VMEM((width, ny, nz), F32),
            pltpu.VMEM((width, ny, nz), F32),
            pltpu.VMEM(warm_fields.shape, F32),
            pltpu.VMEM((1, 4, slots), jnp.int32),
            pltpu.VMEM((8, 128), jnp.int32),
            pltpu.VMEM((n, width + 2, fields, ny, nz), BF16),
            pltpu.VMEM((2, width, ny, nz), F32),
            pltpu.VMEM((fields, width, ny, nz), F32),
            pltpu.VMEM((2, 2, fields, ny, nz), BF16),
            pltpu.VMEM((2, 2, fields, ny, nz), BF16),
            pltpu.VMEM((n, 8, 128), jnp.int32),
            pltpu.SMEM((n, 8, 128), jnp.int32),
            pltpu.SMEM((MEASURE_ROWS_MEAN, 8), jnp.int32),
            pltpu.VMEM((n, fields, width, 3, ny, nz), BF16),
            dma((2,)),
            dma((2,)),
            dma((2, half, 2)),
            dma((2, half, 2)),
            dma((n, 2)),
            dma((n, 2)),
            dma((n,)),
            dma((n,)),
            dma((4,)),
            dma,
        ],
        compiler_params=pltpu.CompilerParams(
            collective_id=0, has_side_effects=True, vmem_limit_bytes=60 * 1024 * 1024
        ),
    )(sigma_real, sigma_imag, warm_fields, quads.transpose(0, 2, 1), locations, counts)


def solution(mesh):
    in_specs = (
        P("space", None, None),
        P("space", None, None),
        P("elec", None, "space", None, None),
        P("elec"),
        P("elec"),
        P("elec", None, None),
    )
    out_specs = P("elec", None, "space", None, None)
    return jax.shard_map(
        functools.partial(per_device, mesh.shape["elec"], mesh.shape["space"]),
        mesh=mesh,
        in_specs=in_specs,
        out_specs=out_specs,
        check_vma=False,
    )
```
